256 devices in a mesh: ep: 64 (over z, y, core), tp: 4 (over x).
Axes of the slice: x: 4, y: 4, z: 8, core: 2. Of those that a mesh axis runs over, the one named last changes fastest.
Arguments:
- tokens: bfloat16 [8192, 4096], P(('ep', 'tp')), may hold values from -6 to 6
- grad_out: bfloat16 [8192, 4096], P(('ep', 'tp')), may hold values from -1 to 1
- expert_ids: int32 [8192, 3], P('ep'), may hold values from 0 to 63, all different within a row; in each aligned block of 32 rows (0 to 31, 32 to 63, ...) at most 2 rows name the same one
- gate_weights: bfloat16 [8192, 3], P('ep'), may hold values from 0.049804688 to 0.5
- w_gate: bfloat16 [64, 4096, 1536], P('ep', None, 'tp'), may hold values from -0.09375 to 0.09375
- w_up: bfloat16 [64, 4096, 1536], P('ep', None, 'tp'), may hold values from -0.09375 to 0.09375
- w_down: bfloat16 [64, 1536, 4096], P('ep', 'tp'), may hold values from -0.15625 to 0.15625
- scale_gate: float32 [64, 32, 12], P('ep', None, 'tp'), may hold values from 0.25 to 2
- scale_up: float32 [64, 32, 12], P('ep', None, 'tp'), may hold values from 0.25 to 2
- scale_down: float32 [64, 12, 32], P('ep', 'tp'), may hold values from 0.25 to 2
Outputs:
- grad_tokens: bfloat16 [8192, 4096], P(('ep', 'tp'))
- grad_gates: float32 [8192, 3], P(('ep', 'tp'))
The draws below stay inside these ranges and needn't reach their ends.
Inputs may be any that keep to these rules, and one draw needn't show every extreme that they name: `expert_ids`: the 3 experts of a row are different. Within each aligned block of 32 rows no expert is named more than 2 times, and in some block one expert is named exactly 2 times.
All inputs are finite; a program needn't handle non-finite values.
Results may differ from the reference program's by a relative error of at most 0.018.
Values may be sent and summed in bfloat16 or wider, within the bound.
No kernel may reach another device: no remote copies, remote signals or barrier semaphores. Data moves between devices by JAX's collectives and lax.ppermute only.
A program may use at most 128 MiB of HBM per device.

```python
import math
import jax
import jax.numpy as jnp
import numpy as np
from jax import lax

D = 4096
HID = 1536
BLOCK = 128
TOP = 3
TOK_EP = 128
EXPERTS = 64
HID_TP = 384
TOKENS = 8192
CAP_Q = 2
CAP = 8
N_EP = 64
N_TP = 4


def shard_levels(own_key, shape, cuts, least, top_value):
    def one(axis_at, blocks):
        heights = jax.random.uniform(jax.random.fold_in(jax.random.fold_in(own_key, 6), axis_at), (blocks,), jnp.float32, least / len(cuts), top_value / len(cuts))
        return jnp.repeat(jnp.exp(heights), shape[axis_at] // blocks).reshape((-1,) + (1,) * (len(shape) - axis_at - 1))

    level = one(*cuts[0])
    for cut in cuts[1:]:
        level = level * one(*cut)
    return level


def shared_out(key, own, number, rows, amount, top, reach, slope):
    ranking = jax.random.permutation(key, amount)
    heavy_load, common = portions_of(amount, rows * top, reach, slope, True), portions_of(amount, rows * top, reach, slope, False)
    places = jnp.arange(amount)

    def named(lengths, turn):
        used = int((lengths > 0).sum())
        fixed = max(1, used // 4)
        passed = fixed + (places - fixed + turn * (used - fixed)) % max(1, amount - fixed)
        return jnp.zeros((amount,), jnp.int32).at[ranking[jnp.where(places < fixed, places, passed)]].set(jnp.asarray(lengths, jnp.int32))

    lengths = jnp.where(number % 4 == 0, named(heavy_load, number // 4), named(common, number - number // 4 - 1))
    mixed = jax.random.permutation(jax.random.fold_in(own, 3), amount)
    giver, sink = mixed[0:amount // 2 * 2:2], mixed[1:amount // 2 * 2:2]
    slack = jnp.minimum(lengths[giver] - 1, reach - lengths[sink]) // 2
    slack = jnp.where((giver == ranking[0]) | (sink == ranking[0]) | (lengths[sink] == 0), 0, jnp.maximum(slack, 0))
    passed = jax.random.randint(jax.random.fold_in(own, 4), (amount // 2,), 0, 1 << 20) % (slack + 1)
    lengths = lengths.at[giver].add(-passed).at[sink].add(passed)
    items = jnp.searchsorted(jnp.cumsum(lengths), jnp.arange(rows * top), side="right").astype(jnp.int32)
    grid = items.reshape(top, rows).T
    grid = grid[jax.random.permutation(jax.random.fold_in(own, 1), rows)]
    turn = jax.random.randint(jax.random.fold_in(own, 2), (rows, 1), 0, top)
    return jnp.take_along_axis(grid, (jnp.arange(top)[None, :] + turn) % top, axis=1)


def portions_of(number_of, total, bound, lean, full):
    portions = [(1 << 20) // math.isqrt(standing ** lean) + 1 for standing in range(1, number_of + 1)]
    largest = bound if full else min(bound, max(-(-total // number_of), total * portions[0] // sum(portions)))
    least = 1 if total - largest >= number_of - 1 else 0
    given, surplus = [largest] + [least] * (number_of - 1), total - largest - least * (number_of - 1)
    while surplus > 0:
        free = [i for i in range(1, number_of) if given[i] < largest] or [i for i in range(1, number_of) if given[i] < bound]
        whole, budget = sum([portions[i] for i in free]), surplus
        for i in free:
            more = min(bound - given[i], max(1, budget * portions[i] // whole), surplus)
            given[i] = given[i] + more
            surplus = surplus - more
    return np.array(given)


def scatter_about(rng, extent, scale, limit, pieces=(), held_as=jnp.bfloat16):
    factor_of = shard_levels(rng, extent, pieces, -0.22, 0.18) if pieces else 1.0
    drawn = jax.random.normal(rng, extent, jnp.float32) * scale * factor_of
    return jnp.minimum(jnp.maximum(drawn, -limit), limit).astype(held_as)


def setup_inputs(seed: int = 0) -> dict:
    seeds = jax.random.split(jax.random.key(seed), 11)
    tokens = scatter_about(seeds[0], (TOKENS, D), 1.0, 6.0, ((0, 256),))
    grad_out = scatter_about(seeds[1], (TOKENS, D), 0.125, 1.0, ((0, 256),))
    expert_ids_keys = jax.random.split(jax.random.fold_in(seeds[2], 1), TOKENS // (TOK_EP // N_TP))
    expert_ids_turns = jax.random.permutation(jax.random.fold_in(seeds[2], 3), TOKENS // (TOK_EP // N_TP))
    expert_ids = jax.vmap(lambda own, number: shared_out(jax.random.fold_in(seeds[2], 2), own, number, TOK_EP // N_TP, EXPERTS, TOP, CAP_Q, 1))(expert_ids_keys, expert_ids_turns).reshape((TOKENS, TOP))
    gate_weights = jnp.clip(jnp.exp(math.log(0.5) - 2.306499 * jax.random.uniform(seeds[3], (TOKENS, TOP), jnp.float32) ** shard_levels(seeds[3], (TOKENS, TOP), ((0, 64),), -0.2, 0.2)), 0.049804688, 0.5).astype(jnp.bfloat16)
    w_gate = scatter_about(seeds[4], (EXPERTS, D, HID), D ** -0.5, 0.09375, ((0, 64), (2, 4)))
    w_up = scatter_about(seeds[5], (EXPERTS, D, HID), D ** -0.5, 0.09375, ((0, 64), (2, 4)))
    w_down = scatter_about(seeds[6], (EXPERTS, HID, D), HID ** -0.5, 0.15625, ((0, 64), (1, 4)))
    scale_gate = jnp.clip(jnp.exp(math.log(2.0) - 2.0794415 * jax.random.uniform(seeds[7], (EXPERTS, D // BLOCK, HID // BLOCK), jnp.float32) ** shard_levels(seeds[7], (EXPERTS, D // BLOCK, HID // BLOCK), ((0, 64), (2, 4)), -0.2, 0.2)), 0.25, 2.0)
    scale_up = jnp.clip(jnp.exp(math.log(2.0) - 2.0794415 * jax.random.uniform(seeds[8], (EXPERTS, D // BLOCK, HID // BLOCK), jnp.float32) ** shard_levels(seeds[8], (EXPERTS, D // BLOCK, HID // BLOCK), ((0, 64), (2, 4)), -0.2, 0.2)), 0.25, 2.0)
    scale_down = jnp.clip(jnp.exp(math.log(2.0) - 2.0794415 * jax.random.uniform(seeds[9], (EXPERTS, HID // BLOCK, D // BLOCK), jnp.float32) ** shard_levels(seeds[9], (EXPERTS, HID // BLOCK, D // BLOCK), ((0, 64), (1, 4)), -0.2, 0.2)), 0.25, 2.0)
    return dict(tokens=tokens, grad_out=grad_out, expert_ids=expert_ids, gate_weights=gate_weights, w_gate=w_gate, w_up=w_up, w_down=w_down, scale_gate=scale_gate, scale_up=scale_up, scale_down=scale_down)


def dequantize(quant, scales):
    rows, cols = quant.shape
    blocks = quant.astype(jnp.float32).reshape(rows // BLOCK, BLOCK, cols // BLOCK, BLOCK)
    return (blocks * scales[:, None, :, None]).reshape(rows, cols).astype(jnp.bfloat16)


def expert_grads(operands):
    rows_in, rows_dy, rows_gate, q_gate, q_up, q_down, s_gate, s_up, s_down = operands
    wgate = dequantize(q_gate, s_gate)
    wupper = dequantize(q_up, s_up)
    wdown = dequantize(q_down, s_down)
    pre = jnp.dot(rows_in, wgate, preferred_element_type=jnp.float32)
    upper = jnp.dot(rows_in, wupper, preferred_element_type=jnp.float32)
    raw = jnp.dot(rows_dy, wdown.T, preferred_element_type=jnp.float32)
    sig = jax.nn.sigmoid(pre)
    act = pre * sig
    hidden = act * upper
    d_hidden = rows_gate.astype(jnp.float32)[:, None] * raw
    d_upper = (d_hidden * act).astype(jnp.bfloat16)
    d_pre = (d_hidden * upper * sig * (1.0 + pre * (1.0 - sig))).astype(jnp.bfloat16)
    total_tok = jnp.zeros((rows_in.shape[0], D), jnp.float32)
    total_gate = jnp.zeros((rows_in.shape[0],), jnp.float32)
    for quarter in range(N_TP):
        lower = quarter * HID_TP
        upper_end = lower + HID_TP
        part_gate = jnp.sum(hidden[:, lower:upper_end] * raw[:, lower:upper_end], axis=1).astype(jnp.bfloat16)
        part_tok = jnp.dot(d_pre[:, lower:upper_end], wgate[:, lower:upper_end].T, preferred_element_type=jnp.float32)
        part_tok = part_tok + jnp.dot(d_upper[:, lower:upper_end], wupper[:, lower:upper_end].T, preferred_element_type=jnp.float32)
        total_tok = total_tok + part_tok.astype(jnp.bfloat16).astype(jnp.float32)
        total_gate = total_gate + part_gate.astype(jnp.float32)
    return total_tok, total_gate


def reference(tokens, grad_out, expert_ids, gate_weights, w_gate, w_up, w_down, scale_gate, scale_up, scale_down):
    grouped = expert_ids.reshape(N_EP, TOK_EP * TOP)
    onehot = (grouped[:, :, None] == jnp.arange(EXPERTS, dtype=jnp.int32)[None, None, :]).astype(jnp.int32)
    rank = jnp.sum(jnp.cumsum(onehot, axis=1) * onehot, axis=2) - 1
    group_index = jnp.arange(N_EP, dtype=jnp.int32)[:, None]
    slot = (grouped * (N_EP * CAP) + group_index * CAP + rank).reshape(-1).astype(jnp.int32)
    token_of = (jnp.arange(TOKENS * TOP, dtype=jnp.int32) // TOP).astype(jnp.int32)
    slots_all = EXPERTS * N_EP * CAP
    buf_in = jnp.zeros((slots_all, D), jnp.bfloat16).at[slot].set(tokens[token_of])
    buf_dy = jnp.zeros((slots_all, D), jnp.bfloat16).at[slot].set(grad_out[token_of])
    buf_gate = jnp.zeros((slots_all,), jnp.bfloat16).at[slot].set(gate_weights.reshape(-1))
    shape_rows = (EXPERTS, N_EP * CAP)
    grads_tok, grads_gate = lax.map(expert_grads, (buf_in.reshape(shape_rows + (D,)), buf_dy.reshape(shape_rows + (D,)), buf_gate.reshape(shape_rows), w_gate, w_up, w_down, scale_gate, scale_up, scale_down))
    grads_tok = grads_tok.reshape(slots_all, D)
    grads_gate = grads_gate.reshape(slots_all)
    slot_pairs = slot.reshape(TOKENS, TOP)
    result = jnp.zeros((TOKENS, D), jnp.float32)
    for choice_k in range(TOP):
        result = result + grads_tok[slot_pairs[:, choice_k]]
    grad_gates = grads_gate[slot].reshape(TOKENS, TOP)
    return result.astype(jnp.bfloat16), grad_gates
```

```python
import functools

import jax
import jax.numpy as jnp
from jax import lax
from jax.experimental import pallas as pl
from jax.experimental.pallas import tpu as pltpu
from jax.sharding import PartitionSpec as P

BF = jnp.bfloat16
F32 = jnp.float32
BLOCK = 128
MIB = 1 << 20
VMEM = pl.BlockSpec(memory_space=pltpu.VMEM)
SMEM = pl.BlockSpec(memory_space=pltpu.SMEM)


def params(mib):
    return pltpu.CompilerParams(vmem_limit_bytes=mib * MIB)


def cost(flops, moved):
    return pl.CostEstimate(flops=flops, bytes_accessed=moved, transcendentals=0)


def dot(a, b, dims=((1,), (0,))):
    return lax.dot_general(a, b, (dims, ((), ())), preferred_element_type=F32)


def pack_kernel(rows, t_ref, ids_ref, gates_ref, x_ref, d_ref, sx_ref, sd_ref, comb_ref, pick_ref):
    t = t_ref[0]
    top, group = ids_ref.shape
    slots = sx_ref.shape[0]
    width = x_ref.shape[1]
    lane = lax.broadcasted_iota(jnp.int32, (slots, group), 0)
    row = lax.broadcasted_iota(jnp.int32, (slots, group), 1)
    expert, copy = lane // 2, lane % 2
    mine = (row // rows) == t
    hits = [(ids_ref[k : k + 1, :] == expert) & mine for k in range(top)]
    member = functools.reduce(jnp.logical_or, hits)
    member = jnp.where(member, 1.0, 0.0).astype(BF)
    before = lax.broadcasted_iota(jnp.int32, (group, group), 0) < lax.broadcasted_iota(
        jnp.int32, (group, group), 1
    )
    prior = dot(member, jnp.where(before, 1.0, 0.0).astype(BF))
    ranked = prior == copy.astype(F32)
    keep = lax.broadcasted_iota(jnp.int32, (group, rows), 0) == t * rows + lax.broadcasted_iota(
        jnp.int32, (group, rows), 1
    )
    keep = jnp.where(keep, 1.0, 0.0).astype(BF)
    weight = jnp.zeros((slots, group), F32)
    send = jnp.zeros((slots, rows), F32)
    for k in range(top):
        hit = jnp.where(hits[k] & ranked, 1.0, 0.0)
        weight = weight + hit * gates_ref[k : k + 1, :].astype(F32)
        picked = dot(hit.astype(BF), keep)
        pick_ref[k] = picked.astype(BF)
        send = send + picked
    comb_ref[...] = dot(keep, weight.astype(BF), ((0,), (1,))).astype(BF)
    send = send.astype(BF)
    step = 1024
    for c in range(0, width, step):
        sx_ref[:, c : c + step] = dot(send, x_ref[:, c : c + step]).astype(BF)
    for c in range(0, width, step):
        sd_ref[:, c : c + step] = dot(send, d_ref[:, c : c + step]).astype(BF)


def prep_kernel(sg_ref, su_ref, sd_ref, wg_ref, wu_ref, wd_ref, both_ref, back_ref, down_ref):
    i = pl.program_id(0)
    depth, hid = wg_ref.shape
    for b in range(depth // BLOCK):
        at = i * (depth // BLOCK) + b
        rs = slice(b * BLOCK, (b + 1) * BLOCK)
        for j in range(hid // BLOCK):
            cs = slice(j * BLOCK, (j + 1) * BLOCK)
            ct = slice(hid + j * BLOCK, hid + (j + 1) * BLOCK)
            g = wg_ref[rs, cs].astype(F32) * sg_ref[at, j]
            u = wu_ref[rs, cs].astype(F32) * su_ref[at, j]
            d = wd_ref[cs, rs].astype(F32) * sd_ref[j, at]
            both_ref[rs, cs] = g.astype(BF)
            both_ref[rs, ct] = u.astype(BF)
            back_ref[cs, rs] = g.T.astype(BF)
            back_ref[ct, rs] = u.T.astype(BF)
            down_ref[rs, cs] = d.T.astype(BF)


def joined(refs):
    return jnp.concatenate([r[...] for r in refs], axis=0)


def forward_kernel(*refs):
    pieces, w_ref, out_ref = refs[:8], refs[8], refs[9]
    part = dot(joined(pieces), w_ref[...])

    @pl.when(pl.program_id(0) == 0)
    def _():
        out_ref[...] = part

    @pl.when(pl.program_id(0) > 0)
    def _():
        out_ref[...] += part


def middle_kernel(*refs):
    pieces, w_ref, pre_ref, d_ref, gate_ref, raw_ref = refs[:8], *refs[8:]
    part = dot(joined(pieces), w_ref[...])

    @pl.when(pl.program_id(0) == 0)
    def _():
        raw_ref[...] = part

    @pl.when(pl.program_id(0) > 0)
    def _():
        raw_ref[...] += part

    @pl.when(pl.program_id(0) == pl.num_programs(0) - 1)
    def _():
        hid = raw_ref.shape[1]
        step = 128
        for r in range(0, raw_ref.shape[0], step):
            rs = slice(r, r + step)
            raw = raw_ref[rs, :]
            pre = pre_ref[rs, :hid]
            up = pre_ref[rs, hid:]
            sig = 1.0 / (1.0 + jnp.exp(-pre))
            act = pre * sig
            total = jnp.sum(act * up * raw, axis=1, keepdims=True)
            d_ref[rs, hid:] = (raw * act).astype(BF)
            d_ref[rs, :hid] = (raw * up * sig * (1.0 + pre * (1.0 - sig))).astype(BF)
            col = lax.broadcasted_iota(jnp.int32, (step, BLOCK), 1)
            gate_ref[rs, :] = jnp.where(col == 0, total, 0.0).astype(BF)


def backward_kernel(has_gate, *refs):
    d_ref, w_ref = refs[:2]
    outs = refs[3:] if has_gate else refs[2:]
    own, rest = outs[0], outs[1:]
    width = w_ref.shape[1]
    step = 512

    def put(rows, cs, value):
        if rows < 128:
            own[rows : rows + 64, cs] = value
        else:
            rest[rows // 64 - 2][:, cs] = value

    for c in range(0, width, step):
        cs = slice(c, c + step)
        part = dot(d_ref[...], w_ref[:, cs]).astype(BF)
        for r in range(0, 512, 64):
            put(r, cs, part[r : r + 64])
    if has_gate:
        cs = slice(width, width + BLOCK)
        for r in range(0, 512, 64):
            put(r, cs, refs[2][r : r + 64, :])


def combine_kernel(comb_ref, pick_ref, *refs):
    backs, tok_ref, gate_ref = refs[:-2], refs[-2], refs[-1]
    at = 0
    comb = comb_ref[...]
    for b in backs:
        width = min(b.shape[1], tok_ref.shape[1] - at)
        tok_ref[:, at : at + width] = dot(comb, b[:, :width]).astype(BF)
        at += width
    sums = backs[-1][:, backs[-1].shape[1] - BLOCK :]
    for k in range(pick_ref.shape[0]):
        gate_ref[k : k + 1, :] = dot(sums, pick_ref[k], ((0,), (0,)))[:1, :]


def ring(n, by):
    return [(i, (i + by) % n) for i in range(n)]


def gather_pieces(x, n):
    h = x.shape[0] // 2
    x1, x2 = x[:h], x[h:]
    right = lambda v: lax.ppermute(v, "tp", ring(n, 1))
    left = lambda v: lax.ppermute(v, "tp", ring(n, -1))
    l1, r2 = right(x1), left(x2)
    l2, r1 = right(x2), left(x1)
    o1, o2 = right(l1), left(r2)
    return [x1, x2, l1, l2, r1, r2, o1, o2]


def scatter_sum(pieces, n):
    own, l1, l2, r1, r2, o1, o2 = pieces
    right = lambda v: lax.ppermute(v, "tp", ring(n, 1))
    left = lambda v: lax.ppermute(v, "tp", ring(n, -1))
    a, b = right(o1), left(o2)
    c2, e1 = right(r2), left(l1)
    c1 = right((r1.astype(F32) + a.astype(F32)).astype(BF))
    e2 = left((l2.astype(F32) + b.astype(F32)).astype(BF))
    h = own.shape[0] // 2
    first = own[:h].astype(F32) + c1.astype(F32) + e1.astype(F32)
    second = own[h:].astype(F32) + c2.astype(F32) + e2.astype(F32)
    return jnp.concatenate([first, second], axis=0).astype(BF)


def exchange(x, experts):
    slots, width = x.shape
    y = lax.all_to_all(
        x.reshape(experts, slots // experts, width), "ep", split_axis=0, concat_axis=0, tiled=True
    )
    return y.reshape(slots, width)


def shards(tokens, grad_out, expert_ids, gate_weights, w_gate, w_up, w_down, scale_gate, scale_up, scale_down):
    n_tp = lax.axis_size("tp")
    experts = lax.axis_size("ep")
    rows, width = tokens.shape
    top = expert_ids.shape[1]
    hid = w_gate.shape[2]
    slots = 2 * experts
    total = n_tp * slots
    t = lax.axis_index("tp").astype(jnp.int32).reshape(1)

    send_in, send_dy, comb, pick = pl.pallas_call(
        functools.partial(pack_kernel, rows),
        in_specs=[SMEM, VMEM, VMEM, VMEM, VMEM],
        out_specs=[VMEM] * 4,
        out_shape=[
            jax.ShapeDtypeStruct((slots, width), BF),
            jax.ShapeDtypeStruct((slots, width), BF),
            jax.ShapeDtypeStruct((rows, slots), BF),
            jax.ShapeDtypeStruct((top, slots, rows), BF),
        ],
        compiler_params=params(24),
        cost_estimate=cost(4 * slots * rows * width, 6 * slots * width),
        name="pack",
    )(t, expert_ids.T, gate_weights.T, tokens, grad_out)

    depth = 512
    steps = width // depth
    both, back, down = pl.pallas_call(
        prep_kernel,
        grid=(steps,),
        in_specs=[
            SMEM,
            SMEM,
            SMEM,
            pl.BlockSpec((depth, hid), lambda i: (i, 0)),
            pl.BlockSpec((depth, hid), lambda i: (i, 0)),
            pl.BlockSpec((hid, depth), lambda i: (0, i)),
        ],
        out_specs=[
            pl.BlockSpec((depth, 2 * hid), lambda i: (i, 0)),
            pl.BlockSpec((2 * hid, depth), lambda i: (0, i)),
            pl.BlockSpec((depth, hid), lambda i: (i, 0)),
        ],
        out_shape=[
            jax.ShapeDtypeStruct((width, 2 * hid), BF),
            jax.ShapeDtypeStruct((2 * hid, width), BF),
            jax.ShapeDtypeStruct((width, hid), BF),
        ],
        compiler_params=params(24),
        cost_estimate=cost(8 * width * hid, 16 * width * hid),
        name="prep",
    )(scale_gate[0], scale_up[0], scale_down[0], w_gate[0], w_up[0], w_down[0])

    x_pieces = gather_pieces(exchange(send_in, experts), n_tp)
    d_pieces = gather_pieces(exchange(send_dy, experts), n_tp)

    piece_specs = [pl.BlockSpec((slots // 2, depth), lambda i: (0, i))] * 8
    pre_up = pl.pallas_call(
        forward_kernel,
        grid=(steps,),
        in_specs=piece_specs + [pl.BlockSpec((depth, 2 * hid), lambda i: (i, 0))],
        out_specs=pl.BlockSpec((total, 2 * hid), lambda i: (0, 0)),
        out_shape=jax.ShapeDtypeStruct((total, 2 * hid), F32),
        compiler_params=params(24),
        cost_estimate=cost(4 * total * width * hid, 4 * width * hid + 2 * total * width),
        name="forward",
    )(*x_pieces, both)

    d_both, part_gate = pl.pallas_call(
        middle_kernel,
        grid=(steps,),
        in_specs=piece_specs
        + [
            pl.BlockSpec((depth, hid), lambda i: (i, 0)),
            pl.BlockSpec((total, 2 * hid), lambda i: (0, 0)),
        ],
        out_specs=[
            pl.BlockSpec((total, 2 * hid), lambda i: (0, 0)),
            pl.BlockSpec((total, BLOCK), lambda i: (0, 0)),
        ],
        out_shape=[
            jax.ShapeDtypeStruct((total, 2 * hid), BF),
            jax.ShapeDtypeStruct((total, BLOCK), BF),
        ],
        scratch_shapes=[pltpu.VMEM((total, hid), F32)],
        compiler_params=params(24),
        cost_estimate=cost(2 * total * width * hid, 2 * width * hid + 2 * total * width),
        name="middle",
    )(*d_pieces, down, pre_up)

    cuts = 2
    part = width // cuts
    returned = []
    for c in range(cuts):
        has_gate = c == cuts - 1
        out_width = part + (BLOCK if has_gate else 0)
        shapes = [slots] + [slots // 2] * 6
        terms = pl.pallas_call(
            functools.partial(backward_kernel, has_gate),
            grid=(1,),
            in_specs=[
                pl.BlockSpec((total, 2 * hid), lambda i: (0, 0)),
                pl.BlockSpec((2 * hid, part), lambda i, c=c: (0, c)),
            ]
            + ([pl.BlockSpec((total, BLOCK), lambda i: (0, 0))] if has_gate else []),
            out_specs=[pl.BlockSpec((s, out_width), lambda i: (0, 0)) for s in shapes],
            out_shape=[jax.ShapeDtypeStruct((s, out_width), BF) for s in shapes],
            compiler_params=params(24),
            cost_estimate=cost(4 * total * part * hid, 4 * part * hid + 2 * total * part),
            name="backward",
        )(*([d_both, back] + ([part_gate] if has_gate else [])))
        returned.append(exchange(scatter_sum(terms, n_tp), experts))

    grad_rows, grad_gates = pl.pallas_call(
        combine_kernel,
        in_specs=[VMEM] * (2 + cuts),
        out_specs=[VMEM, VMEM],
        out_shape=[
            jax.ShapeDtypeStruct((rows, width), BF),
            jax.ShapeDtypeStruct((top, rows), F32),
        ],
        compiler_params=params(16),
        cost_estimate=cost(2 * slots * rows * width, 3 * slots * width),
        name="combine",
    )(comb, pick, *returned)
    return grad_rows, grad_gates.T


def solution(mesh):
    return jax.shard_map(
        shards,
        mesh=mesh,
        in_specs=(
            P(("ep", "tp"), None),
            P(("ep", "tp"), None),
            P("ep", None),
            P("ep", None),
            P("ep", None, "tp"),
            P("ep", None, "tp"),
            P("ep", "tp", None),
            P("ep", None, "tp"),
            P("ep", None, "tp"),
            P("ep", "tp", None),
        ),
        out_specs=(P(("ep", "tp"), None), P(("ep", "tp"), None)),
        check_vma=False,
    )
```

```python
import functools

import jax
import jax.numpy as jnp
from jax import lax
from jax.experimental import pallas as pl
from jax.experimental.pallas import tpu as pltpu
from jax.sharding import PartitionSpec as P

BF = jnp.bfloat16
F32 = jnp.float32
BLOCK = 128
VMEM_MIB = 56
SPAN = 2048
MIB = 1 << 20
VMEM = pl.BlockSpec(memory_space=pltpu.VMEM)
SMEM = pl.BlockSpec(memory_space=pltpu.SMEM)


def params(mib):
    return pltpu.CompilerParams(vmem_limit_bytes=mib * MIB)


def cost(flops, moved):
    return pl.CostEstimate(flops=flops, bytes_accessed=moved, transcendentals=0)


def dot(a, b, dims=((1,), (0,))):
    return lax.dot_general(a, b, (dims, ((), ())), preferred_element_type=F32)


def pack_kernel(rows, t_ref, ids_ref, gates_ref, x_ref, d_ref, sa_ref, comb_ref, pick_ref, place_ref):
    t = t_ref[0]
    top, group = ids_ref.shape
    experts = sa_ref.shape[0]
    slots = 2 * experts
    width = x_ref.shape[1]
    quarters = group // rows
    lane = lax.broadcasted_iota(jnp.int32, (slots, group), 0)
    expert, copy = lane % experts, lane // experts
    hits = [ids_ref[k : k + 1, :] == expert for k in range(top)]
    member = functools.reduce(jnp.logical_or, hits)
    member = jnp.where(member, 1.0, 0.0).astype(BF)
    first = lax.broadcasted_iota(jnp.int32, (group, group), 0)
    later = lax.broadcasted_iota(jnp.int32, (group, group), 1)
    before = (first < later) & (first // rows == later // rows)
    prior = dot(member, jnp.where(before, 1.0, 0.0).astype(BF))
    ranked = prior == copy.astype(F32)

    def keep(quarter):
        at = lax.broadcasted_iota(jnp.int32, (group, rows), 0)
        own = quarter * rows + lax.broadcasted_iota(jnp.int32, (group, rows), 1)
        return jnp.where(at == own, 1.0, 0.0).astype(BF)

    mine = keep(t)
    weight = jnp.zeros((slots, group), F32)
    every = jnp.zeros((slots, group), F32)
    for k in range(top):
        hit = jnp.where(hits[k] & ranked, 1.0, 0.0)
        weight = weight + hit * gates_ref[k : k + 1, :].astype(F32)
        pick_ref[k] = dot(hit.astype(BF), mine).astype(BF)
        every = every + hit
    comb_ref[...] = dot(mine, weight.astype(BF), ((0,), (1,))).astype(BF)
    every = every.astype(BF)
    for q, off in enumerate((0, quarters - 1, 1, quarters // 2)):
        place_ref[q] = dot(every[experts:], keep(lax.rem(t + off, quarters))).astype(BF)
    send = dot(every, mine).astype(BF)
    step = 1024
    for c in range(0, width, step):
        moved = dot(send, x_ref[:, c : c + step]).astype(BF)
        sa_ref[:, c : c + step] = moved[:experts]
        sa_ref[:, 2 * width + c : 2 * width + c + step] = moved[experts:]
        sa_ref[:, width + c : width + c + step] = dot(send[:experts], d_ref[:, c : c + step]).astype(BF)


def place_kernel(place_ref, *refs):
    pieces, out_ref = refs[:-1], refs[-1]
    width = pieces[0].shape[1]
    step = 1024
    for q, piece in enumerate(pieces):
        for c in range(0, width, step):
            moved = dot(place_ref[q], piece[:, c : c + step]).astype(BF)
            out_ref[:, q * width + c : q * width + c + step] = moved


def prep_kernel(sg_ref, su_ref, sd_ref, wg_ref, wu_ref, wd_ref, both_ref, back_ref, down_ref):
    i = pl.program_id(0)
    depth, hid = wg_ref.shape
    for b in range(depth // BLOCK):
        at = i * (depth // BLOCK) + b
        rs = slice(b * BLOCK, (b + 1) * BLOCK)
        for j in range(hid // BLOCK):
            cs = slice(j * BLOCK, (j + 1) * BLOCK)
            ct = slice(hid + j * BLOCK, hid + (j + 1) * BLOCK)
            g = wg_ref[rs, cs].astype(F32) * sg_ref[at, j]
            u = wu_ref[rs, cs].astype(F32) * su_ref[at, j]
            d = wd_ref[cs, rs].astype(F32) * sd_ref[j, at]
            both_ref[rs, cs] = g.astype(BF)
            both_ref[rs, ct] = u.astype(BF)
            back_ref[cs, rs] = g.T.astype(BF)
            back_ref[ct, rs] = u.T.astype(BF)
            down_ref[rs, cs] = d.T.astype(BF)


def joined(refs):
    return jnp.concatenate([r[...] for r in refs], axis=0)


def expert_kernel(pieces, steps, d_pieces, *refs):
    x_refs, refs = refs[:pieces], refs[pieces:]
    d_refs, refs = refs[:d_pieces], refs[d_pieces:]
    both_ref, down_ref, back_ref = refs[:3]
    outs = refs[3:-4]
    pre_ref, raw_ref, made_ref, gate_ref = refs[-4:]
    i = pl.program_id(0)
    hid = raw_ref.shape[1]

    @pl.when(i < steps)
    def _():
        pre = dot(joined(x_refs), both_ref[...])
        raw = dot(joined(d_refs), down_ref[...])

        @pl.when(i == 0)
        def _():
            pre_ref[...] = pre
            raw_ref[...] = raw

        @pl.when(i > 0)
        def _():
            pre_ref[...] += pre
            raw_ref[...] += raw

    @pl.when(i == steps)
    def _():
        step = 64
        for r in range(0, raw_ref.shape[0], step):
            rs = slice(r, r + step)
            raw = raw_ref[rs, :]
            pre = pre_ref[rs, :hid]
            up = pre_ref[rs, hid:]
            sig = 1.0 / (1.0 + jnp.exp(-pre))
            act = pre * sig
            total = jnp.sum(act * up * raw, axis=1, keepdims=True)
            made_ref[rs, hid:] = (raw * act).astype(BF)
            made_ref[rs, :hid] = (raw * up * sig * (1.0 + pre * (1.0 - sig))).astype(BF)
            col = lax.broadcasted_iota(jnp.int32, (step, BLOCK), 1)
            gate_ref[rs, :] = jnp.where(col == 0, total, 0.0).astype(BF)

    @pl.when(i >= steps)
    def _():
        def put(cs, value):
            at = 0
            for o in outs:
                o[:, cs] = value[at : at + o.shape[0]]
                at += o.shape[0]

        width = back_ref.shape[1]
        step = 512
        for c in range(0, width, step):
            cs = slice(c, c + step)
            put(cs, dot(made_ref[...], back_ref[:, cs]).astype(BF))
        put(slice(width, width + BLOCK), gate_ref[...])


def combine_kernel(comb_ref, pick_ref, a_ref, b_ref, tok_ref, gate_ref):
    experts = a_ref.shape[0]
    comb = comb_ref[...]
    half = tok_ref.shape[1] // 2
    step = 1024
    for h in range(2):
        for c in range(0, half, step):
            cs = slice(h * (half + BLOCK) + c, h * (half + BLOCK) + c + step)
            back = jnp.concatenate([a_ref[:, cs], b_ref[:, cs]], axis=0)
            tok_ref[:, h * half + c : h * half + c + step] = dot(comb, back).astype(BF)
    sums = jnp.concatenate([a_ref[:, half : half + BLOCK], b_ref[:, half : half + BLOCK]], axis=0)
    for k in range(pick_ref.shape[0]):
        gate_ref[k : k + 1, :] = dot(sums, pick_ref[k], ((0,), (0,)))[:1, :]


def ring(n, by):
    return [(i, (i + by) % n) for i in range(n)]


def to_right(v, n):
    return lax.ppermute(v, "tp", ring(n, 1))


def to_left(v, n):
    return lax.ppermute(v, "tp", ring(n, -1))


def across(v, n):
    return lax.ppermute(v, "tp", ring(n, n // 2))


def gather(x, n, direct):
    left, right = to_right(x, n), to_left(x, n)
    if direct:
        return [x, left, right, across(x, n)]
    h = x.shape[0] // 2
    return [x, left, right, to_right(left[:h], n), to_left(right[h:], n)]


def home(terms, n):
    return home_sum(home_sends(terms, n))


def home_sends(terms, n):
    own, left, right, opposite = terms
    return [own, to_left(left, n), to_right(right, n), across(opposite, n)]


def home_sum(parts):
    return sum(p.astype(F32) for p in parts).astype(BF)


def exchange(x):
    rows, width = x.shape
    y = lax.all_to_all(x.reshape(rows, 2, width // 2), "ep", split_axis=0, concat_axis=0, tiled=True)
    return y.reshape(rows, width)


def shards(tokens, grad_out, expert_ids, gate_weights, w_gate, w_up, w_down, scale_gate, scale_up, scale_down):
    n_tp = lax.axis_size("tp")
    experts = lax.axis_size("ep")
    rows, width = tokens.shape
    top = expert_ids.shape[1]
    hid = w_gate.shape[2]
    slots = 2 * experts
    t = lax.axis_index("tp").astype(jnp.int32).reshape(1)

    send_a, comb, pick, place = pl.pallas_call(
        functools.partial(pack_kernel, rows),
        in_specs=[SMEM, VMEM, VMEM, VMEM, VMEM],
        out_specs=[VMEM] * 4,
        out_shape=[
            jax.ShapeDtypeStruct((experts, 3 * width), BF),
            jax.ShapeDtypeStruct((rows, slots), BF),
            jax.ShapeDtypeStruct((top, slots, rows), BF),
            jax.ShapeDtypeStruct((n_tp, experts, rows), BF),
        ],
        compiler_params=params(58),
        cost_estimate=cost(4 * slots * rows * width, 6 * slots * width),
        name="pack",
    )(t, expert_ids.T, gate_weights.T, tokens, grad_out)

    send_d = pl.pallas_call(
        place_kernel,
        in_specs=[VMEM] * (1 + n_tp),
        out_specs=VMEM,
        out_shape=jax.ShapeDtypeStruct((experts, n_tp * width), BF),
        compiler_params=params(58),
        cost_estimate=cost(2 * n_tp * experts * rows * width, 3 * n_tp * experts * width),
        name="place",
    )(place, *gather(grad_out, n_tp, True))

    depth = 512
    steps = width // depth
    both, back, down = pl.pallas_call(
        prep_kernel,
        grid=(steps,),
        in_specs=[
            SMEM,
            SMEM,
            SMEM,
            pl.BlockSpec((depth, hid), lambda i: (i, 0)),
            pl.BlockSpec((depth, hid), lambda i: (i, 0)),
            pl.BlockSpec((hid, depth), lambda i: (0, i)),
        ],
        out_specs=[
            pl.BlockSpec((depth, 2 * hid), lambda i: (i, 0)),
            pl.BlockSpec((2 * hid, depth), lambda i: (0, i)),
            pl.BlockSpec((depth, hid), lambda i: (i, 0)),
        ],
        out_shape=[
            jax.ShapeDtypeStruct((width, 2 * hid), BF),
            jax.ShapeDtypeStruct((2 * hid, width), BF),
            jax.ShapeDtypeStruct((width, hid), BF),
        ],
        compiler_params=params(58),
        cost_estimate=cost(8 * width * hid, 16 * width * hid),
        name="prep",
    )(scale_gate[0], scale_up[0], scale_down[0], w_gate[0], w_up[0], w_down[0])

    count = n_tp * experts
    span = SPAN
    turns = width // span
    last = turns - 1

    def products(x_pieces, d_pieces, heights):
        pieces = list(x_pieces) + list(d_pieces)

        def spec(piece):
            array, column = piece
            return pl.BlockSpec(
                (array.shape[0], span), lambda i: (0, column // span + jnp.minimum(i, last))
            )

        return pl.pallas_call(
            functools.partial(expert_kernel, len(x_pieces), turns, len(d_pieces)),
            grid=(turns + 2,),
            in_specs=[spec(p) for p in pieces]
            + [
                pl.BlockSpec((span, 2 * hid), lambda i: (jnp.minimum(i, last), 0)),
                pl.BlockSpec((span, hid), lambda i: (jnp.minimum(i, last), 0)),
                pl.BlockSpec((2 * hid, width // 2), lambda i: (0, jnp.maximum(i - turns, 0))),
            ],
            out_specs=[
                pl.BlockSpec((h, width // 2 + BLOCK), lambda i: (0, jnp.maximum(i - turns, 0)))
                for h in heights
            ],
            out_shape=[jax.ShapeDtypeStruct((h, width + 2 * BLOCK), BF) for h in heights],
            scratch_shapes=[
                pltpu.VMEM((count, 2 * hid), F32),
                pltpu.VMEM((count, hid), F32),
                pltpu.VMEM((count, 2 * hid), BF),
                pltpu.VMEM((count, BLOCK), BF),
            ],
            compiler_params=params(VMEM_MIB),
            cost_estimate=cost(10 * count * width * hid, 10 * width * hid + 6 * count * width),
            name="products",
        )(*[array for array, _ in pieces], both, down, back)

    send_d = send_d.reshape(experts, n_tp, width)
    rows_in, send_d, both, back, down = lax.optimization_barrier(
        (exchange(send_a), send_d, both, back, down)
    )
    pieces_a = gather(rows_in[:, : 2 * width], n_tp, False)
    rows_b, *pieces_a[3:] = lax.optimization_barrier((rows_in[:, 2 * width :], *pieces_a[3:]))
    pieces_b = gather(rows_b, n_tp, True)
    rows_d = lax.all_to_all(send_d, "ep", split_axis=0, concat_axis=0, tiled=True)
    rows_d = rows_d.reshape(experts, n_tp * width)
    terms_a = products(
        [(p, 0) for p in pieces_a], [(p, width) for p in pieces_a], [experts] * n_tp
    )
    sent_a = home_sends(terms_a, n_tp)
    first, *pieces_b, rows_d = lax.optimization_barrier((terms_a[0], *pieces_b, rows_d))
    terms_b = products(
        [(p, 0) for p in pieces_b], [(rows_d, q * width) for q in range(n_tp)], [experts] * n_tp
    )
    home_a = home_sum([first, *sent_a[1:]])
    home_a, *terms_b = lax.optimization_barrier((home_a, *terms_b))
    home_b = home(terms_b, n_tp)
    back_a, back_b = exchange(home_a), exchange(home_b)

    grad_rows, grad_gates = pl.pallas_call(
        combine_kernel,
        in_specs=[VMEM] * 4,
        out_specs=[VMEM, VMEM],
        out_shape=[
            jax.ShapeDtypeStruct((rows, width), BF),
            jax.ShapeDtypeStruct((top, rows), F32),
        ],
        compiler_params=params(VMEM_MIB),
        cost_estimate=cost(2 * slots * rows * width, 3 * slots * width),
        name="combine",
    )(comb, pick, back_a, back_b)
    return grad_rows, grad_gates.T


def solution(mesh):
    return jax.shard_map(
        shards,
        mesh=mesh,
        in_specs=(
            P(("ep", "tp"), None),
            P(("ep", "tp"), None),
            P("ep", None),
            P("ep", None),
            P("ep", None, "tp"),
            P("ep", None, "tp"),
            P("ep", "tp", None),
            P("ep", None, "tp"),
            P("ep", None, "tp"),
            P("ep", "tp", None),
        ),
        out_specs=(P(("ep", "tp"), None), P(("ep", "tp"), None)),
        check_vma=False,
    )
```

```python
import functools

import jax
import jax.numpy as jnp
from jax import lax
from jax.experimental import pallas as pl
from jax.experimental.pallas import tpu as pltpu
from jax.sharding import PartitionSpec as P

BF = jnp.bfloat16
F32 = jnp.float32
BLOCK = 128
VMEM_MIB = 44
SPAN = 2048
MIB = 1 << 20
VMEM = pl.BlockSpec(memory_space=pltpu.VMEM)
SMEM = pl.BlockSpec(memory_space=pltpu.SMEM)


def params(mib):
    return pltpu.CompilerParams(vmem_limit_bytes=mib * MIB)


def cost(flops, moved):
    return pl.CostEstimate(flops=flops, bytes_accessed=moved, transcendentals=0)


def dot(a, b, dims=((1,), (0,))):
    return lax.dot_general(a, b, (dims, ((), ())), preferred_element_type=F32)


def pack_kernel(rows, t_ref, ids_ref, gates_ref, x_ref, d_ref, sa_ref, comb_ref, pick_ref, place_ref):
    t = t_ref[0]
    top, group = ids_ref.shape
    experts = sa_ref.shape[0]
    slots = 2 * experts
    width = x_ref.shape[1]
    quarters = group // rows
    lane = lax.broadcasted_iota(jnp.int32, (slots, group), 0)
    expert, copy = lane % experts, lane // experts
    hits = [ids_ref[k : k + 1, :] == expert for k in range(top)]
    member = functools.reduce(jnp.logical_or, hits)
    member = jnp.where(member, 1.0, 0.0).astype(BF)
    first = lax.broadcasted_iota(jnp.int32, (group, group), 0)
    later = lax.broadcasted_iota(jnp.int32, (group, group), 1)
    before = (first < later) & (first // rows == later // rows)
    prior = dot(member, jnp.where(before, 1.0, 0.0).astype(BF))
    ranked = prior == copy.astype(F32)

    def keep(quarter):
        at = lax.broadcasted_iota(jnp.int32, (group, rows), 0)
        own = quarter * rows + lax.broadcasted_iota(jnp.int32, (group, rows), 1)
        return jnp.where(at == own, 1.0, 0.0).astype(BF)

    mine = keep(t)
    weight = jnp.zeros((slots, group), F32)
    every = jnp.zeros((slots, group), F32)
    for k in range(top):
        hit = jnp.where(hits[k] & ranked, 1.0, 0.0)
        weight = weight + hit * gates_ref[k : k + 1, :].astype(F32)
        pick_ref[k] = dot(hit.astype(BF), mine).astype(BF)
        every = every + hit
    comb_ref[...] = dot(mine, weight.astype(BF), ((0,), (1,))).astype(BF)
    every = every.astype(BF)
    for q, off in enumerate((0, quarters - 1, 1, quarters // 2)):
        place_ref[q] = dot(every[experts:], keep(lax.rem(t + off, quarters))).astype(BF)
    send = dot(every, mine).astype(BF)
    step = 1024
    for c in range(0, width, step):
        moved = dot(send, x_ref[:, c : c + step]).astype(BF)
        sa_ref[:, c : c + step] = moved[:experts]
        sa_ref[:, 2 * width + c : 2 * width + c + step] = moved[experts:]
        sa_ref[:, width + c : width + c + step] = dot(send[:experts], d_ref[:, c : c + step]).astype(BF)


def place_kernel(place_ref, *refs):
    pieces, out_ref = refs[:-1], refs[-1]
    width = pieces[0].shape[1]
    step = 1024
    for q, piece in enumerate(pieces):
        for c in range(0, width, step):
            moved = dot(place_ref[q], piece[:, c : c + step]).astype(BF)
            out_ref[:, q * width + c : q * width + c + step] = moved


def prep_kernel(sg_ref, su_ref, sd_ref, wg_ref, wu_ref, wd_ref, both_ref, back_ref, down_ref):
    i = pl.program_id(0)
    depth, hid = wg_ref.shape
    for b in range(depth // BLOCK):
        at = i * (depth // BLOCK) + b
        rs = slice(b * BLOCK, (b + 1) * BLOCK)
        for j in range(hid // BLOCK):
            cs = slice(j * BLOCK, (j + 1) * BLOCK)
            ct = slice(hid + j * BLOCK, hid + (j + 1) * BLOCK)
            g = wg_ref[rs, cs].astype(F32) * sg_ref[at, j]
            u = wu_ref[rs, cs].astype(F32) * su_ref[at, j]
            d = wd_ref[cs, rs].astype(F32) * sd_ref[j, at]
            both_ref[rs, cs] = g.astype(BF)
            both_ref[rs, ct] = u.astype(BF)
            back_ref[cs, rs] = g.T.astype(BF)
            back_ref[ct, rs] = u.T.astype(BF)
            down_ref[rs, cs] = d.T.astype(BF)


def joined(refs):
    return jnp.concatenate([r[...] for r in refs], axis=0)


def expert_kernel(pieces, steps, d_pieces, *refs):
    x_refs, refs = refs[:pieces], refs[pieces:]
    d_refs, refs = refs[:d_pieces], refs[d_pieces:]
    both_ref, down_ref, back_ref = refs[:3]
    outs = refs[3:-4]
    pre_ref, raw_ref, made_ref, gate_ref = refs[-4:]
    i = pl.program_id(0)
    hid = raw_ref.shape[1]

    @pl.when(i < steps)
    def _():
        pre = dot(joined(x_refs), both_ref[...])
        raw = dot(joined(d_refs), down_ref[...])

        @pl.when(i == 0)
        def _():
            pre_ref[...] = pre
            raw_ref[...] = raw

        @pl.when(i > 0)
        def _():
            pre_ref[...] += pre
            raw_ref[...] += raw

    @pl.when(i == steps)
    def _():
        step = 64
        for r in range(0, raw_ref.shape[0], step):
            rs = slice(r, r + step)
            raw = raw_ref[rs, :]
            pre = pre_ref[rs, :hid]
            up = pre_ref[rs, hid:]
            sig = 1.0 / (1.0 + jnp.exp(-pre))
            act = pre * sig
            total = jnp.sum(act * up * raw, axis=1, keepdims=True)
            made_ref[rs, hid:] = (raw * act).astype(BF)
            made_ref[rs, :hid] = (raw * up * sig * (1.0 + pre * (1.0 - sig))).astype(BF)
            col = lax.broadcasted_iota(jnp.int32, (step, BLOCK), 1)
            gate_ref[rs, :] = jnp.where(col == 0, total, 0.0).astype(BF)

    @pl.when(i >= steps)
    def _():
        def put(cs, value):
            at = 0
            for o in outs:
                o[:, cs] = value[at : at + o.shape[0]]
                at += o.shape[0]

        width = back_ref.shape[1]
        step = 512
        for c in range(0, width, step):
            cs = slice(c, c + step)
            put(cs, dot(made_ref[...], back_ref[:, cs]).astype(BF))
        put(slice(width, width + BLOCK), gate_ref[...])


def combine_kernel(comb_ref, pick_ref, a_ref, b_ref, tok_ref, gate_ref):
    experts = a_ref.shape[0]
    comb = comb_ref[...]
    half = tok_ref.shape[1] // 2
    step = 1024
    for h in range(2):
        for c in range(0, half, step):
            cs = slice(h * (half + BLOCK) + c, h * (half + BLOCK) + c + step)
            back = jnp.concatenate([a_ref[:, cs], b_ref[:, cs]], axis=0)
            tok_ref[:, h * half + c : h * half + c + step] = dot(comb, back).astype(BF)
    sums = jnp.concatenate([a_ref[:, half : half + BLOCK], b_ref[:, half : half + BLOCK]], axis=0)
    for k in range(pick_ref.shape[0]):
        gate_ref[k : k + 1, :] = dot(sums, pick_ref[k], ((0,), (0,)))[:1, :]


def ring(n, by):
    return [(i, (i + by) % n) for i in range(n)]


def to_right(v, n):
    return lax.ppermute(v, "tp", ring(n, 1))


def to_left(v, n):
    return lax.ppermute(v, "tp", ring(n, -1))


def across(v, n):
    return lax.ppermute(v, "tp", ring(n, n // 2))


def gather(x, n, direct):
    left, right = to_right(x, n), to_left(x, n)
    if direct:
        return [x, left, right, across(x, n)]
    h, q = x.shape[0] // 2, x.shape[0] // 4
    first = [to_right(left[:q], n), to_left(right[h : h + q], n)]
    second = [to_right(left[q:h], n), to_left(right[h + q :], n)]
    return [x, left, right, first[0], second[0], first[1], second[1]]


def home(terms, n):
    return home_sum(home_sends(terms, n))


def home_sends(terms, n):
    own, left, right, opposite = terms
    return [own, to_left(left, n), to_right(right, n), across(opposite, n)]


def home_sum(parts):
    return sum(p.astype(F32) for p in parts).astype(BF)


def exchange(x):
    rows, width = x.shape
    y = lax.all_to_all(x.reshape(rows, 2, width // 2), "ep", split_axis=0, concat_axis=0, tiled=True)
    return y.reshape(rows, width)


def shards(tokens, grad_out, expert_ids, gate_weights, w_gate, w_up, w_down, scale_gate, scale_up, scale_down):
    n_tp = lax.axis_size("tp")
    experts = lax.axis_size("ep")
    rows, width = tokens.shape
    top = expert_ids.shape[1]
    hid = w_gate.shape[2]
    slots = 2 * experts
    t = lax.axis_index("tp").astype(jnp.int32).reshape(1)

    send_a, comb, pick, place = pl.pallas_call(
        functools.partial(pack_kernel, rows),
        in_specs=[SMEM, VMEM, VMEM, VMEM, VMEM],
        out_specs=[VMEM] * 4,
        out_shape=[
            jax.ShapeDtypeStruct((experts, 3 * width), BF),
            jax.ShapeDtypeStruct((rows, slots), BF),
            jax.ShapeDtypeStruct((top, slots, rows), BF),
            jax.ShapeDtypeStruct((n_tp, experts, rows), BF),
        ],
        compiler_params=params(58),
        cost_estimate=cost(4 * slots * rows * width, 6 * slots * width),
        name="pack",
    )(t, expert_ids.T, gate_weights.T, tokens, grad_out)

    send_d = pl.pallas_call(
        place_kernel,
        in_specs=[VMEM] * (1 + n_tp),
        out_specs=VMEM,
        out_shape=jax.ShapeDtypeStruct((experts, n_tp * width), BF),
        compiler_params=params(58),
        cost_estimate=cost(2 * n_tp * experts * rows * width, 3 * n_tp * experts * width),
        name="place",
    )(place, *gather(grad_out, n_tp, True))

    depth = 512
    steps = width // depth
    both, back, down = pl.pallas_call(
        prep_kernel,
        grid=(steps,),
        in_specs=[
            SMEM,
            SMEM,
            SMEM,
            pl.BlockSpec((depth, hid), lambda i: (i, 0)),
            pl.BlockSpec((depth, hid), lambda i: (i, 0)),
            pl.BlockSpec((hid, depth), lambda i: (0, i)),
        ],
        out_specs=[
            pl.BlockSpec((depth, 2 * hid), lambda i: (i, 0)),
            pl.BlockSpec((2 * hid, depth), lambda i: (0, i)),
            pl.BlockSpec((depth, hid), lambda i: (i, 0)),
        ],
        out_shape=[
            jax.ShapeDtypeStruct((width, 2 * hid), BF),
            jax.ShapeDtypeStruct((2 * hid, width), BF),
            jax.ShapeDtypeStruct((width, hid), BF),
        ],
        compiler_params=params(58),
        cost_estimate=cost(8 * width * hid, 16 * width * hid),
        name="prep",
    )(scale_gate[0], scale_up[0], scale_down[0], w_gate[0], w_up[0], w_down[0])

    count = n_tp * experts
    span = SPAN
    turns = width // span
    last = turns - 1

    def products(x_pieces, d_pieces, heights):
        pieces = list(x_pieces) + list(d_pieces)

        def spec(piece):
            array, column = piece
            return pl.BlockSpec(
                (array.shape[0], span), lambda i: (0, column // span + jnp.minimum(i, last))
            )

        return pl.pallas_call(
            functools.partial(expert_kernel, len(x_pieces), turns, len(d_pieces)),
            grid=(turns + 2,),
            in_specs=[spec(p) for p in pieces]
            + [
                pl.BlockSpec((span, 2 * hid), lambda i: (jnp.minimum(i, last), 0)),
                pl.BlockSpec((span, hid), lambda i: (jnp.minimum(i, last), 0)),
                pl.BlockSpec((2 * hid, width // 2), lambda i: (0, jnp.maximum(i - turns, 0))),
            ],
            out_specs=[
                pl.BlockSpec((h, width // 2 + BLOCK), lambda i: (0, jnp.maximum(i - turns, 0)))
                for h in heights
            ],
            out_shape=[jax.ShapeDtypeStruct((h, width + 2 * BLOCK), BF) for h in heights],
            scratch_shapes=[
                pltpu.VMEM((count, 2 * hid), F32),
                pltpu.VMEM((count, hid), F32),
                pltpu.VMEM((count, 2 * hid), BF),
                pltpu.VMEM((count, BLOCK), BF),
            ],
            compiler_params=params(VMEM_MIB),
            cost_estimate=cost(10 * count * width * hid, 10 * width * hid + 6 * count * width),
            name="products",
        )(*[array for array, _ in pieces], both, down, back)

    send_d = send_d.reshape(experts, n_tp, width)
    rows_in, send_d, both, back, down = lax.optimization_barrier(
        (exchange(send_a), send_d, both, back, down)
    )
    pieces_a = gather(rows_in[:, : 2 * width], n_tp, False)
    rows_b, pieces_a[3], pieces_a[5] = lax.optimization_barrier(
        (rows_in[:, 2 * width :], pieces_a[3], pieces_a[5])
    )
    pieces_b = gather(rows_b, n_tp, True)
    rows_d = lax.all_to_all(send_d, "ep", split_axis=0, concat_axis=0, tiled=True)
    rows_d = rows_d.reshape(experts, n_tp * width)
    terms_a = products(
        [(p, 0) for p in pieces_a], [(p, width) for p in pieces_a], [experts] * n_tp
    )
    sent_a = home_sends(terms_a, n_tp)
    first, *pieces_b, rows_d = lax.optimization_barrier((terms_a[0], *pieces_b, rows_d))
    terms_b = products(
        [(p, 0) for p in pieces_b], [(rows_d, q * width) for q in range(n_tp)], [experts] * n_tp
    )
    home_a = home_sum([first, *sent_a[1:]])
    home_a, *terms_b = lax.optimization_barrier((home_a, *terms_b))
    home_b = home(terms_b, n_tp)
    back_a, back_b = exchange(home_a), exchange(home_b)

    grad_rows, grad_gates = pl.pallas_call(
        combine_kernel,
        in_specs=[VMEM] * 4,
        out_specs=[VMEM, VMEM],
        out_shape=[
            jax.ShapeDtypeStruct((rows, width), BF),
            jax.ShapeDtypeStruct((top, rows), F32),
        ],
        compiler_params=params(VMEM_MIB),
        cost_estimate=cost(2 * slots * rows * width, 3 * slots * width),
        name="combine",
    )(comb, pick, back_a, back_b)
    return grad_rows, grad_gates.T


def solution(mesh):
    return jax.shard_map(
        shards,
        mesh=mesh,
        in_specs=(
            P(("ep", "tp"), None),
            P(("ep", "tp"), None),
            P("ep", None),
            P("ep", None),
            P("ep", None, "tp"),
            P("ep", None, "tp"),
            P("ep", "tp", None),
            P("ep", None, "tp"),
            P("ep", None, "tp"),
            P("ep", "tp", None),
        ),
        out_specs=(P(("ep", "tp"), None), P(("ep", "tp"), None)),
        check_vma=False,
    )
```

```python
import functools

import jax
import jax.numpy as jnp
from jax import lax
from jax.experimental import pallas as pl
from jax.experimental.pallas import tpu as pltpu
from jax.sharding import PartitionSpec as P

BF = jnp.bfloat16
F32 = jnp.float32
BLOCK = 128
VMEM_MIB = 44
SPAN = 2048
MIB = 1 << 20
VMEM = pl.BlockSpec(memory_space=pltpu.VMEM)
SMEM = pl.BlockSpec(memory_space=pltpu.SMEM)


def params(mib):
    return pltpu.CompilerParams(vmem_limit_bytes=mib * MIB)


def cost(flops, moved):
    return pl.CostEstimate(flops=flops, bytes_accessed=moved, transcendentals=0)


def dot(a, b, dims=((1,), (0,))):
    return lax.dot_general(a, b, (dims, ((), ())), preferred_element_type=F32)


def pack_kernel(rows, t_ref, ids_ref, gates_ref, x_ref, d_ref, sa_ref, comb_ref, pick_ref, place_ref):
    t = t_ref[0]
    top, group = ids_ref.shape
    experts = sa_ref.shape[0]
    slots = 2 * experts
    width = x_ref.shape[1]
    quarters = group // rows
    lane = lax.broadcasted_iota(jnp.int32, (slots, group), 0)
    expert, copy = lane % experts, lane // experts
    hits = [ids_ref[k : k + 1, :] == expert for k in range(top)]
    member = functools.reduce(jnp.logical_or, hits)
    member = jnp.where(member, 1.0, 0.0).astype(BF)
    first = lax.broadcasted_iota(jnp.int32, (group, group), 0)
    later = lax.broadcasted_iota(jnp.int32, (group, group), 1)
    before = (first < later) & (first // rows == later // rows)
    prior = dot(member, jnp.where(before, 1.0, 0.0).astype(BF))
    ranked = prior == copy.astype(F32)

    def keep(quarter):
        at = lax.broadcasted_iota(jnp.int32, (group, rows), 0)
        own = quarter * rows + lax.broadcasted_iota(jnp.int32, (group, rows), 1)
        return jnp.where(at == own, 1.0, 0.0).astype(BF)

    mine = keep(t)
    weight = jnp.zeros((slots, group), F32)
    every = jnp.zeros((slots, group), F32)
    for k in range(top):
        hit = jnp.where(hits[k] & ranked, 1.0, 0.0)
        weight = weight + hit * gates_ref[k : k + 1, :].astype(F32)
        pick_ref[k] = dot(hit.astype(BF), mine).astype(BF)
        every = every + hit
    comb_ref[...] = dot(mine, weight.astype(BF), ((0,), (1,))).astype(BF)
    every = every.astype(BF)
    for q, off in enumerate((0, quarters - 1, 1, quarters // 2)):
        place_ref[q] = dot(every[experts:], keep(lax.rem(t + off, quarters))).astype(BF)
    send = dot(every, mine).astype(BF)
    step = 1024
    half = sa_ref.shape[2]

    def put(at, value):
        sa_ref[:, at // half, at % half : at % half + step] = value

    for c in range(0, width, step):
        moved = dot(send, x_ref[:, c : c + step]).astype(BF)
        put(c, moved[:experts])
        put(2 * width + c, moved[experts:])
        put(width + c, dot(send[:experts], d_ref[:, c : c + step]).astype(BF))


def place_kernel(place_ref, *refs):
    pieces, out_ref = refs[:-1], refs[-1]
    width = pieces[0].shape[1]
    step = 1024
    for q, piece in enumerate(pieces):
        for c in range(0, width, step):
            moved = dot(place_ref[q], piece[:, c : c + step]).astype(BF)
            out_ref[:, q * width + c : q * width + c + step] = moved


def prep_kernel(sg_ref, su_ref, sd_ref, wg_ref, wu_ref, wd_ref, both_ref, back_ref, down_ref):
    i = pl.program_id(0)
    depth, hid = wg_ref.shape
    for b in range(depth // BLOCK):
        at = i * (depth // BLOCK) + b
        rs = slice(b * BLOCK, (b + 1) * BLOCK)
        for j in range(hid // BLOCK):
            cs = slice(j * BLOCK, (j + 1) * BLOCK)
            ct = slice(hid + j * BLOCK, hid + (j + 1) * BLOCK)
            g = wg_ref[rs, cs].astype(F32) * sg_ref[at, j]
            u = wu_ref[rs, cs].astype(F32) * su_ref[at, j]
            d = wd_ref[cs, rs].astype(F32) * sd_ref[j, at]
            both_ref[rs, cs] = g.astype(BF)
            both_ref[rs, ct] = u.astype(BF)
            back_ref[cs, rs] = g.T.astype(BF)
            back_ref[ct, rs] = u.T.astype(BF)
            down_ref[rs, cs] = d.T.astype(BF)


def joined(refs):
    return jnp.concatenate([r[...] for r in refs], axis=0)


def expert_kernel(pieces, steps, d_pieces, *refs):
    x_refs, refs = refs[:pieces], refs[pieces:]
    d_refs, refs = refs[:d_pieces], refs[d_pieces:]
    both_ref, down_ref, back_ref = refs[:3]
    outs = refs[3:-4]
    pre_ref, raw_ref, made_ref, gate_ref = refs[-4:]
    i = pl.program_id(0)
    hid = raw_ref.shape[1]

    @pl.when(i < steps)
    def _():
        pre = dot(joined(x_refs), both_ref[...])
        raw = dot(joined(d_refs), down_ref[...])

        @pl.when(i == 0)
        def _():
            pre_ref[...] = pre
            raw_ref[...] = raw

        @pl.when(i > 0)
        def _():
            pre_ref[...] += pre
            raw_ref[...] += raw

    @pl.when(i == steps)
    def _():
        step = 64
        for r in range(0, raw_ref.shape[0], step):
            rs = slice(r, r + step)
            raw = raw_ref[rs, :]
            pre = pre_ref[rs, :hid]
            up = pre_ref[rs, hid:]
            sig = 1.0 / (1.0 + jnp.exp(-pre))
            act = pre * sig
            total = jnp.sum(act * up * raw, axis=1, keepdims=True)
            made_ref[rs, hid:] = (raw * act).astype(BF)
            made_ref[rs, :hid] = (raw * up * sig * (1.0 + pre * (1.0 - sig))).astype(BF)
            col = lax.broadcasted_iota(jnp.int32, (step, BLOCK), 1)
            gate_ref[rs, :] = jnp.where(col == 0, total, 0.0).astype(BF)

    @pl.when(i >= steps)
    def _():
        def put(cs, value):
            at = 0
            for o in outs:
                o[:, cs] = value[at : at + o.shape[0]]
                at += o.shape[0]

        width = back_ref.shape[1]
        step = 512
        for c in range(0, width, step):
            cs = slice(c, c + step)
            put(cs, dot(made_ref[...], back_ref[:, cs]).astype(BF))
        put(slice(width, width + BLOCK), gate_ref[...])


def combine_kernel(comb_ref, pick_ref, a_ref, b_ref, tok_ref, gate_ref):
    experts = a_ref.shape[0]
    comb = comb_ref[...]
    half = tok_ref.shape[1] // 2
    step = 1024
    for h in range(2):
        for c in range(0, half, step):
            cs = slice(h * (half + BLOCK) + c, h * (half + BLOCK) + c + step)
            back = jnp.concatenate([a_ref[:, cs], b_ref[:, cs]], axis=0)
            tok_ref[:, h * half + c : h * half + c + step] = dot(comb, back).astype(BF)
    sums = jnp.concatenate([a_ref[:, half : half + BLOCK], b_ref[:, half : half + BLOCK]], axis=0)
    for k in range(pick_ref.shape[0]):
        gate_ref[k : k + 1, :] = dot(sums, pick_ref[k], ((0,), (0,)))[:1, :]


def ring(n, by):
    return [(i, (i + by) % n) for i in range(n)]


def to_right(v, n):
    return lax.ppermute(v, "tp", ring(n, 1))


def to_left(v, n):
    return lax.ppermute(v, "tp", ring(n, -1))


def across(v, n):
    return lax.ppermute(v, "tp", ring(n, n // 2))


def gather(x, n, direct):
    left, right = to_right(x, n), to_left(x, n)
    if direct:
        return [x, left, right, across(x, n)]
    h, q = x.shape[0] // 2, x.shape[0] // 4
    first = [to_right(left[:q], n), to_left(right[h : h + q], n)]
    second = [to_right(left[q:h], n), to_left(right[h + q :], n)]
    return [x, left, right, first[0], second[0], first[1], second[1]]


def home(terms, n):
    return home_sum(home_sends(terms, n))


def home_sends(terms, n):
    own, left, right, opposite = terms
    return [own, to_left(left, n), to_right(right, n), across(opposite, n)]


def home_sum(parts):
    return sum(p.astype(F32) for p in parts).astype(BF)


def exchange(x):
    rows, width = x.shape
    y = lax.all_to_all(x.reshape(rows, 2, width // 2), "ep", split_axis=0, concat_axis=0, tiled=True)
    return y.reshape(rows, width)


def shards(tokens, grad_out, expert_ids, gate_weights, w_gate, w_up, w_down, scale_gate, scale_up, scale_down):
    n_tp = lax.axis_size("tp")
    experts = lax.axis_size("ep")
    rows, width = tokens.shape
    top = expert_ids.shape[1]
    hid = w_gate.shape[2]
    slots = 2 * experts
    t = lax.axis_index("tp").astype(jnp.int32).reshape(1)

    send_a, comb, pick, place = pl.pallas_call(
        functools.partial(pack_kernel, rows),
        in_specs=[SMEM, VMEM, VMEM, VMEM, VMEM],
        out_specs=[VMEM] * 4,
        out_shape=[
            jax.ShapeDtypeStruct((experts, 2, 3 * width // 2), BF),
            jax.ShapeDtypeStruct((rows, slots), BF),
            jax.ShapeDtypeStruct((top, slots, rows), BF),
            jax.ShapeDtypeStruct((n_tp, experts, rows), BF),
        ],
        compiler_params=params(58),
        cost_estimate=cost(4 * slots * rows * width, 6 * slots * width),
        name="pack",
    )(t, expert_ids.T, gate_weights.T, tokens, grad_out)

    send_d = pl.pallas_call(
        place_kernel,
        in_specs=[VMEM] * (1 + n_tp),
        out_specs=VMEM,
        out_shape=jax.ShapeDtypeStruct((experts, n_tp * width), BF),
        compiler_params=params(58),
        cost_estimate=cost(2 * n_tp * experts * rows * width, 3 * n_tp * experts * width),
        name="place",
    )(place, *gather(grad_out, n_tp, True))

    depth = 512
    steps = width // depth
    both, back, down = pl.pallas_call(
        prep_kernel,
        grid=(steps,),
        in_specs=[
            SMEM,
            SMEM,
            SMEM,
            pl.BlockSpec((depth, hid), lambda i: (i, 0)),
            pl.BlockSpec((depth, hid), lambda i: (i, 0)),
            pl.BlockSpec((hid, depth), lambda i: (0, i)),
        ],
        out_specs=[
            pl.BlockSpec((depth, 2 * hid), lambda i: (i, 0)),
            pl.BlockSpec((2 * hid, depth), lambda i: (0, i)),
            pl.BlockSpec((depth, hid), lambda i: (i, 0)),
        ],
        out_shape=[
            jax.ShapeDtypeStruct((width, 2 * hid), BF),
            jax.ShapeDtypeStruct((2 * hid, width), BF),
            jax.ShapeDtypeStruct((width, hid), BF),
        ],
        compiler_params=params(58),
        cost_estimate=cost(8 * width * hid, 16 * width * hid),
        name="prep",
    )(scale_gate[0], scale_up[0], scale_down[0], w_gate[0], w_up[0], w_down[0])

    count = n_tp * experts
    span = SPAN
    turns = width // span
    last = turns - 1

    def products(x_pieces, d_pieces, heights):
        pieces = list(x_pieces) + list(d_pieces)

        def spec(piece):
            array, column = piece
            return pl.BlockSpec(
                (array.shape[0], span), lambda i: (0, column // span + jnp.minimum(i, last))
            )

        return pl.pallas_call(
            functools.partial(expert_kernel, len(x_pieces), turns, len(d_pieces)),
            grid=(turns + 2,),
            in_specs=[spec(p) for p in pieces]
            + [
                pl.BlockSpec((span, 2 * hid), lambda i: (jnp.minimum(i, last), 0)),
                pl.BlockSpec((span, hid), lambda i: (jnp.minimum(i, last), 0)),
                pl.BlockSpec((2 * hid, width // 2), lambda i: (0, jnp.maximum(i - turns, 0))),
            ],
            out_specs=[
                pl.BlockSpec((h, width // 2 + BLOCK), lambda i: (0, jnp.maximum(i - turns, 0)))
                for h in heights
            ],
            out_shape=[jax.ShapeDtypeStruct((h, width + 2 * BLOCK), BF) for h in heights],
            scratch_shapes=[
                pltpu.VMEM((count, 2 * hid), F32),
                pltpu.VMEM((count, hid), F32),
                pltpu.VMEM((count, 2 * hid), BF),
                pltpu.VMEM((count, BLOCK), BF),
            ],
            compiler_params=params(VMEM_MIB),
            cost_estimate=cost(10 * count * width * hid, 10 * width * hid + 6 * count * width),
            name="products",
        )(*[array for array, _ in pieces], both, down, back)

    send_d = send_d.reshape(experts, n_tp, width)
    rows_in = lax.all_to_all(send_a, "ep", split_axis=0, concat_axis=0, tiled=True)
    rows_in = rows_in.reshape(experts, 3 * width)
    rows_in, send_d, both, back, down = lax.optimization_barrier(
        (rows_in, send_d, both, back, down)
    )
    pieces_a = gather(rows_in[:, : 2 * width], n_tp, False)
    rows_b, pieces_a[3], pieces_a[5] = lax.optimization_barrier(
        (rows_in[:, 2 * width :], pieces_a[3], pieces_a[5])
    )
    pieces_b = gather(rows_b, n_tp, True)
    rows_d = lax.all_to_all(send_d, "ep", split_axis=0, concat_axis=0, tiled=True)
    rows_d = rows_d.reshape(experts, n_tp * width)
    terms_a = products(
        [(p, 0) for p in pieces_a], [(p, width) for p in pieces_a], [experts] * n_tp
    )
    sent_a = home_sends(terms_a, n_tp)
    first, *pieces_b, rows_d = lax.optimization_barrier((terms_a[0], *pieces_b, rows_d))
    terms_b = products(
        [(p, 0) for p in pieces_b], [(rows_d, q * width) for q in range(n_tp)], [experts] * n_tp
    )
    home_a = home_sum([first, *sent_a[1:]])
    home_a, *terms_b = lax.optimization_barrier((home_a, *terms_b))
    home_b = home(terms_b, n_tp)
    back_a, back_b = exchange(home_a), exchange(home_b)

    grad_rows, grad_gates = pl.pallas_call(
        combine_kernel,
        in_specs=[VMEM] * 4,
        out_specs=[VMEM, VMEM],
        out_shape=[
            jax.ShapeDtypeStruct((rows, width), BF),
            jax.ShapeDtypeStruct((top, rows), F32),
        ],
        compiler_params=params(VMEM_MIB),
        cost_estimate=cost(2 * slots * rows * width, 3 * slots * width),
        name="combine",
    )(comb, pick, back_a, back_b)
    return grad_rows, grad_gates.T


def solution(mesh):
    return jax.shard_map(
        shards,
        mesh=mesh,
        in_specs=(
            P(("ep", "tp"), None),
            P(("ep", "tp"), None),
            P("ep", None),
            P("ep", None),
            P("ep", None, "tp"),
            P("ep", None, "tp"),
            P("ep", "tp", None),
            P("ep", None, "tp"),
            P("ep", None, "tp"),
            P("ep", "tp", None),
        ),
        out_specs=(P(("ep", "tp"), None), P(("ep", "tp"), None)),
        check_vma=False,
    )
```
